512 devices in a mesh: tm: 64 (over y, x, core), head: 8 (over z).
Axes of the slice: x: 4, y: 8, z: 8, core: 2. Of those that a mesh axis runs over, the one named last changes fastest.
Arguments:
- queries: bfloat16 [8192, 1024], P('tm', 'head'), may hold values from -5.2 to 5.2
- keys: bfloat16 [8192, 1024], P('tm', 'head'), may hold values from -5.2 to 5.2
- values: bfloat16 [8192, 1024], P('tm', 'head'), may hold values from -24 to 24
- out_weight: bfloat16 [5120, 1024], P(None, 'head'), may hold values from -0.1875 to 0.1875
- output_cotangent: bfloat16 [8192, 5120], P('tm'), may hold values from -6 to 6
- block_mask: int32 [64, 64], replicated, may hold values from 0 to 1, as said below
- segment_of_device: int32 [64], replicated, may hold values from 0 to 63, each once
Outputs:
- layer_output: bfloat16 [8192, 5120], P('tm', 'head')
- query_grad: bfloat16 [8192, 1024], P('tm', 'head')
- key_grad: bfloat16 [8192, 1024], P('tm', 'head')
- value_grad: bfloat16 [8192, 1024], P('tm', 'head')
The draws below stay inside these ranges and needn't reach their ends.
Inputs may be any that keep to these rules, and one draw needn't show every extreme that they name: block_mask[i, j] = 1 lets the queries of sequence block i (128 tokens) see the keys of block j; two blocks of one latent frame (1024 tokens) always see each other; for frames further apart each query block sees a band of key blocks of the other frame whose width halves with the distance level, at least one block. Rows i * 128 to (i + 1) * 128 - 1 of every token-indexed array hold the sequence's segment segment_of_device[i] of 128 tokens; each segment appears once.
All inputs are finite; a program needn't handle non-finite values.
Results may differ from the reference program's by a relative error of at most 0.04.
Values may be sent and summed in bfloat16 or wider, within the bound.
A program may use at most 64 MiB of HBM per device.

```python
import math
import jax
import jax.numpy as jnp
from jax import lax

D = 5120
HD = 128
BLK = 128
FRAME = 1024
TOK_DEV = 128
TOKENS = 8192
HEADS = 8
N_TM = 64


def draw_queries(key, part):
    key = jax.random.fold_in(key, 1)
    return jnp.clip(1.3 * jax.random.normal(key, (TOKENS, HEADS * HD), jnp.float32), -5.2, 5.2).astype(jnp.bfloat16)


def draw_keys(key, part):
    key = jax.random.fold_in(key, 2)
    return jnp.clip(1.3 * jax.random.normal(key, (TOKENS, HEADS * HD), jnp.float32), -5.2, 5.2).astype(jnp.bfloat16)


def draw_block_mask(key, part):
    key = jax.random.fold_in(key, 3)
    total_blocks = TOKENS // BLK
    frame_blocks = FRAME // BLK
    frame_count = TOKENS // FRAME
    block_index = jnp.arange(total_blocks, dtype=jnp.int32)
    frame_of = block_index // frame_blocks
    offset_of = block_index % frame_blocks
    distance = jnp.abs(frame_of[:, None] - frame_of[None, :])
    levels = (distance >= 1).astype(jnp.int32) + (distance >= 3).astype(jnp.int32) + (distance >= 7).astype(jnp.int32)
    widths = jnp.maximum(jnp.right_shift(jnp.full(levels.shape, frame_blocks, jnp.int32), levels), 1)
    shift_table = jax.random.randint(key, (frame_count, frame_count), 0, frame_blocks)
    shifts = shift_table[frame_of[:, None], frame_of[None, :]]
    band_offset = (offset_of[None, :] - offset_of[:, None] - shifts + 2 * frame_blocks) % frame_blocks
    kept_blocks = (band_offset < widths) | (distance == 0)
    return kept_blocks.astype(jnp.int32)


def block_levels(key, dims, shards, least, high):
    gain, own = 1.0, jax.random.fold_in(key, 6)
    for dim, shards_of in shards:
        steps = jnp.exp(jax.random.uniform(jax.random.fold_in(own, dim), (shards_of,), jnp.float32, least / len(shards), high / len(shards)))
        gain = gain * jnp.repeat(steps, dims[dim] // shards_of).reshape([-1 if axis == dim else 1 for axis in range(len(dims))])
    return gain


def centred(stream_key, shape, deviation, bound, cuts=(), held_as=jnp.bfloat16):
    factor_of = block_levels(stream_key, shape, cuts, -0.22, 0.18) if cuts else 1.0
    result = jax.random.normal(stream_key, shape, jnp.float32) * deviation * factor_of
    return jnp.minimum(jnp.maximum(result, -bound), bound).astype(held_as)


def setup_inputs(seed: int = 0) -> dict:
    key_of = jax.random.split(jax.random.key(seed), 8)
    queries = draw_queries(jax.random.fold_in(key_of[7], 71), 0)
    keys = draw_keys(jax.random.fold_in(key_of[7], 71), 0)
    values = centred(key_of[2], (TOKENS, HEADS * HD), 4.0, 24.0, ((0, 64), (1, 8)))
    out_weight = centred(key_of[3], (D, HEADS * HD), (HEADS * HD) ** -0.5, 0.1875, ((1, 8),))
    output_cotangent = centred(key_of[4], (TOKENS, D), 1.0, 6.0, ((0, 64),))
    block_mask = draw_block_mask(jax.random.fold_in(key_of[7], 71), 0)
    segment_of_device = jax.random.permutation(key_of[6], N_TM).astype(jnp.int32)
    return {"queries": queries, "keys": keys, "values": values, "out_weight": out_weight, "output_cotangent": output_cotangent, "block_mask": block_mask, "segment_of_device": segment_of_device}


MASKED_SCORE = -1e+30

def reference(queries, keys, values, out_weight, output_cotangent, block_mask, segment_of_device):
    score_scale = 1.0 / math.sqrt(HD)
    row_index = jnp.arange(TOKENS, dtype=jnp.int32)
    position = segment_of_device[row_index // TOK_DEV] * TOK_DEV + row_index % TOK_DEV
    blocks = (position // BLK).astype(jnp.int32)
    block_rows = math.gcd(TOKENS, 1024)
    pieces = TOKENS // block_rows

    def per_head(running, head_index):
        first = (head_index * HD).astype(jnp.int32)
        query_h = lax.dynamic_slice_in_dim(queries, first, HD, 1)
        key_h = lax.dynamic_slice_in_dim(keys, first, HD, 1)
        value_h = lax.dynamic_slice_in_dim(values, first, HD, 1)
        weight_h = lax.dynamic_slice_in_dim(out_weight, first, HD, 1)

        def query_links(piece):
            rows_blocks = lax.dynamic_slice_in_dim(blocks, (piece * block_rows).astype(jnp.int32), block_rows, 0)
            return block_mask[rows_blocks][:, blocks] == 1

        def forward_block(piece):
            query_rows = lax.dynamic_slice_in_dim(query_h, (piece * block_rows).astype(jnp.int32), block_rows, 0)
            linked = query_links(piece)
            scores = jnp.where(linked, jnp.dot(query_rows, key_h.T, preferred_element_type=jnp.float32) * score_scale, MASKED_SCORE)
            row_top = lax.optimization_barrier(jnp.max(scores, axis=1))
            totals = lax.optimization_barrier(jnp.sum(jnp.where(linked, jnp.exp(scores - row_top[:, None]), 0.0), axis=1))
            row_lse = row_top + jnp.log(totals)
            weights = jnp.exp(scores - row_lse[:, None]).astype(jnp.bfloat16)
            attended = jnp.dot(weights, value_h, preferred_element_type=jnp.float32).astype(jnp.bfloat16)
            return (attended, row_lse)
        attended, row_lse = lax.map(forward_block, jnp.arange(pieces, dtype=jnp.int32))
        attended = attended.reshape(TOKENS, HD)
        row_lse = row_lse.reshape(TOKENS)
        attended = lax.optimization_barrier(attended)
        term = lax.optimization_barrier(jnp.dot(attended, weight_h.T, preferred_element_type=jnp.float32).astype(jnp.bfloat16))
        running = running + term.astype(jnp.float32)
        out_grad = lax.optimization_barrier(jnp.dot(output_cotangent, weight_h, preferred_element_type=jnp.float32).astype(jnp.bfloat16))
        row_delta = lax.optimization_barrier(jnp.sum(out_grad.astype(jnp.float32) * attended.astype(jnp.float32), axis=1))

        def query_block(piece):
            first_row = (piece * block_rows).astype(jnp.int32)
            query_rows = lax.dynamic_slice_in_dim(query_h, first_row, block_rows, 0)
            grad_rows = lax.dynamic_slice_in_dim(out_grad, first_row, block_rows, 0)
            lse_rows = lax.dynamic_slice_in_dim(row_lse, first_row, block_rows, 0)
            delta_rows = lax.dynamic_slice_in_dim(row_delta, first_row, block_rows, 0)
            linked = query_links(piece)
            scores = jnp.where(linked, jnp.dot(query_rows, key_h.T, preferred_element_type=jnp.float32) * score_scale, MASKED_SCORE)
            exact_probs = jnp.exp(scores - lse_rows[:, None])
            slopes = jnp.dot(grad_rows, value_h.T, preferred_element_type=jnp.float32)
            score_grad = (exact_probs * (slopes - delta_rows[:, None])).astype(jnp.bfloat16)
            return (jnp.dot(score_grad, key_h, preferred_element_type=jnp.float32) * score_scale).astype(jnp.bfloat16)

        def key_block(piece):
            first_row = (piece * block_rows).astype(jnp.int32)
            key_rows = lax.dynamic_slice_in_dim(key_h, first_row, block_rows, 0)
            value_rows = lax.dynamic_slice_in_dim(value_h, first_row, block_rows, 0)
            column_blocks = lax.dynamic_slice_in_dim(blocks, first_row, block_rows, 0)
            linked = block_mask[blocks][:, column_blocks] == 1
            scores = jnp.where(linked, jnp.dot(query_h, key_rows.T, preferred_element_type=jnp.float32) * score_scale, MASKED_SCORE)
            exact_probs = jnp.exp(scores - row_lse[:, None])
            slopes = jnp.dot(out_grad, value_rows.T, preferred_element_type=jnp.float32)
            score_grad = (exact_probs * (slopes - row_delta[:, None])).astype(jnp.bfloat16)
            weights = exact_probs.astype(jnp.bfloat16)
            key_grad = (jnp.dot(score_grad.T, query_h, preferred_element_type=jnp.float32) * score_scale).astype(jnp.bfloat16)
            value_grad = jnp.dot(weights.T, out_grad, preferred_element_type=jnp.float32).astype(jnp.bfloat16)
            return (key_grad, value_grad)
        query_grad = lax.map(query_block, jnp.arange(pieces, dtype=jnp.int32)).reshape(TOKENS, HD)
        key_grad, value_grad = lax.map(key_block, jnp.arange(pieces, dtype=jnp.int32))
        return (running, (query_grad, key_grad.reshape(TOKENS, HD), value_grad.reshape(TOKENS, HD)))
    start = jnp.zeros((TOKENS, D), jnp.float32)
    running, grads = lax.scan(per_head, start, jnp.arange(HEADS, dtype=jnp.int32))

    def join_heads(stacked):
        return jnp.transpose(stacked, (1, 0, 2)).reshape(TOKENS, HEADS * HD)
    return (running.astype(jnp.bfloat16), join_heads(grads[0]), join_heads(grads[1]), join_heads(grads[2]))
```

```python
import functools
import math

import jax
import jax.numpy as jnp
from jax import lax
from jax.experimental import pallas as pl
from jax.experimental.pallas import tpu as pltpu
from jax.sharding import PartitionSpec as P

HD = 128
NX, NY = 4, 8
BLOCKS = 2 * NX * NY
MASKED_SCORE = -1e30
SCALE = 1.0 / math.sqrt(HD)
SCALE2 = SCALE * math.log2(math.e)
MESH = pl.DeviceIdType.MESH
BF, F32 = jnp.bfloat16, jnp.float32

DX = (0, 1, -1, 2)


def nt(left, right):
    return lax.dot_general(left, right, (((1,), (1,)), ((), ())), preferred_element_type=F32)


def nn(left, right):
    return lax.dot_general(left, right, (((1,), (0,)), ((), ())), preferred_element_type=F32)


def kernel(nz, ow, q_hbm, k_hbm, v_hbm, w_hbm, cot_hbm, mask_ref, seg_ref, out_ref, dq_ref, dk_ref, dv_ref,
           ka, vb, qa, ob, s_scr, p_scr, w_own, cot, w_all, att, stat, lsem, ssem, rsem):
    t, z = lax.axis_index("tm"), lax.axis_index("head")
    y, x, c = t // (2 * NX), (t // 2) % NX, t % 2

    def at(dx=0, dy=0, core=0, dz=0):
        col, row = (x + (dx + NX)) % NX, (y + (dy + NY)) % NY
        return ((row * NX + col) * 2 + (c + core) % 2, (z + dz) % nz)

    right, left, across = at(dx=1), at(dx=-1), at(dx=2)
    up, down, sib = at(dy=1), at(dy=-1), at(core=1)

    loads = []

    def load(src, dst):
        cp = pltpu.make_async_copy(src, dst, lsem.at[len(loads)])
        cp.start()
        loads.append(cp)
        return cp

    l_k, l_v, l_q = load(k_hbm, ka.at[0]), load(v_hbm, vb.at[0]), load(q_hbm, qa.at[0])
    l_w, l_c = load(w_hbm, w_own), load(cot_hbm, cot)

    partners = [at(dx=dx, core=cc) for cc in (0, 1) for dx in DX][1:]
    partners += [at(dy=dy) for dy in range(1, NY)] + [at(dz=dz) for dz in range(1, nz)]
    barrier = pltpu.get_barrier_semaphore()
    for who in partners:
        pl.semaphore_signal(barrier, inc=1, device_id=who, device_id_type=MESH)

    l_w.wait()
    l_c.wait()
    grad = nn(cot[...], w_own[...]).astype(BF)
    ob[0] = grad
    l_k.wait()
    l_v.wait()
    l_q.wait()
    pl.semaphore_wait(barrier, len(partners))

    sent = []

    def send(src, dst, who):
        i = len(sent)
        cp = pltpu.make_async_remote_copy(
            src_ref=src, dst_ref=dst, send_sem=ssem.at[i], recv_sem=rsem.at[i], device_id=who, device_id_type=MESH
        )
        cp.start()
        sent.append(cp)
        return cp

    def arrive(*copies):
        for cp in copies:
            cp.wait_recv()

    def rows(buf, i, n):
        return buf.at[pl.ds(i, n)]

    class A:
        def __init__(self, buf):
            self.buf, self.sib = buf, []
            self.line = [send(buf.at[0], buf.at[i], who) for i, who in ((2, right), (1, left), (3, across))]

        def first(self):
            arrive(*self.line)
            b = self.buf
            self.y = [send(rows(b, 0, 4), rows(b, 12, 4), up), send(rows(b, 0, 4), rows(b, 8, 4), down)]

        def wave(self, p):
            arrive(*self.y)
            b, g = self.buf, 8 * p
            if p < 3:
                self.y = [send(rows(b, g + 4, 4), rows(b, g + 12, 4), up), send(rows(b, g, 4), rows(b, g + 8, 4), down)]
            else:
                self.y = [send(rows(b, g + 4, 2), rows(b, 4, 2), up), send(rows(b, g + 2, 2), rows(b, 6, 2), down)]
            self.sib.append(send(rows(b, g, 8), rows(b, 32 + g, 8), sib))

        def last(self):
            arrive(*self.y)
            self.sib.append(send(rows(self.buf, 0, 8), rows(self.buf, 32, 8), sib))

    class B:
        def __init__(self, buf):
            self.buf, self.sib, self.x, self.x2 = buf, [], {}, {}
            b = buf
            self.y = [send(b.at[0], b.at[9], up), send(b.at[0], b.at[8], down)]
            self.x[0] = [send(b.at[0], b.at[4], right), send(b.at[0], b.at[2], left)]

        def wave(self, p):
            arrive(*self.y)
            b, g = self.buf, 8 * p
            if p < 3:
                self.y = [send(b.at[g + 1], b.at[g + 9], up), send(b.at[g], b.at[g + 8], down)]
            elif p == 3:
                top, low = pl.ds(0, 64), pl.ds(64, 64)
                self.y = [send(b.at[g + 1, top], b.at[1, top], up), send(b.at[g, low], b.at[1, low], down)]
            if p < 4:
                self.x[p] = [send(rows(b, g, 2), rows(b, g + 4, 2), right), send(rows(b, g, 2), rows(b, g + 2, 2), left)]
            else:
                self.x[p] = [send(b.at[1], b.at[5], right), send(b.at[1], b.at[3], left)]

        def relay(self, p):
            arrive(*self.x[p])
            b, g = self.buf, 8 * p
            if 1 <= p <= 3:
                self.x2[p] = [send(b.at[g + 4], b.at[g + 6], right), send(b.at[g + 3], b.at[g + 7], left)]
            else:
                k = p // 4
                top, low = pl.ds(0, 64), pl.ds(64, 64)
                self.x2[p] = [
                    send(b.at[4 + k, top], b.at[6 + k, top], right),
                    send(b.at[2 + k, low], b.at[6 + k, low], left),
                ]

        def share(self, p):
            arrive(*self.x2[p])
            if p == 0:
                arrive(*self.x2[4])
            self.sib.append(send(rows(self.buf, 8 * p, 8), rows(self.buf, 32 + 8 * p, 8), sib))

    vals, keys = B(vb), A(ka)
    ques, grads = A(qa), B(ob)
    half = ow // 2
    part = pl.ds(pl.multiple_of(c * half, 16), half)
    w_in = []
    for dz in range(1, nz):
        first = pl.multiple_of(((z + nz - dz) % nz) * ow + c * half, 16)
        w_in.append(send(w_own.at[pl.ds(first, half)], w_all.at[dz, part], at(dz=-dz + nz)))

    own_seg = seg_ref[t]

    def place(g, dxi):
        core, p, k = g // 8, (g // 2) % 4, g % 2
        dy = jnp.where(p == 0, 4 * k, jnp.where(k == 0, p, NY - p))
        col, row = (x + (DX[dxi] + NX)) % NX, (y + dy) % NY
        return seg_ref[(row * NX + col) * 2 + (c + core) % 2]

    def bias_of(link):
        return (1 - link).astype(F32) * MASKED_SCORE

    def chunk_a(buf, g):
        return buf[pl.ds(g * 4, 4)].reshape(4 * HD, HD)

    def chunk_b(buf, g):
        base = (g // 2) * 8 + g % 2
        return jnp.concatenate([buf[base + 2 * dxi] for dxi in range(4)], axis=0)

    def over(body, init, groups):
        for first, count in groups:
            init = lax.fori_loop(0, count, lambda i, v: body(first + i, v), init)
        return init

    q_own = qa[0]

    def score(g, top):
        s = nt(q_own, chunk_a(ka, g))
        for b in range(4):
            tile = s[:, b * HD:(b + 1) * HD] * SCALE2 + bias_of(mask_ref[own_seg, place(g, b)])
            s_scr[g * 4 + b] = tile
            top = jnp.maximum(top, tile)
        return top

    top = jnp.full((HD, HD), MASKED_SCORE, F32)

    keys.first()
    vals.wave(1)
    vals.relay(0)
    top = over(score, top, [(0, 1)])
    keys.wave(1)
    vals.wave(2)
    vals.relay(1)
    top = over(score, top, [(2, 2)])
    keys.wave(2)
    vals.wave(3)
    vals.relay(2)
    vals.share(1)
    ques.first()
    grads.wave(1)
    grads.relay(0)
    arrive(keys.sib[0])
    top = over(score, top, [(4, 2), (10, 2)])
    keys.wave(3)
    vals.wave(4)
    vals.relay(3)
    vals.share(2)
    vals.relay(4)
    arrive(keys.sib[1])
    top = over(score, top, [(6, 2), (12, 2)])
    keys.last()
    ques.wave(1)
    grads.wave(2)
    grads.relay(1)
    vals.share(3)
    vals.share(0)
    arrive(keys.sib[2], keys.sib[3])
    top = over(score, top, [(1, 1), (14, 2), (8, 2)])
    row_top = jnp.max(top, axis=1, keepdims=True)
    w_sib = []
    for dz in range(1, nz):
        arrive(w_in[dz - 1])
        w_sib.append(send(w_all.at[dz, part], w_all.at[dz, part], sib))
    arrive(*vals.sib)

    def weigh(g, carry):
        total, attended = carry
        tiles = []
        for b in range(4):
            p = jnp.exp2(s_scr[g * 4 + b] - row_top)
            total = total + p
            tiles.append(p.astype(BF))
            p_scr[g * 4 + b] = tiles[-1]
        return total, attended + nn(jnp.concatenate(tiles, axis=1), chunk_b(vb, g))

    zero = jnp.zeros((HD, HD), F32)
    total, attended = over(weigh, (zero, zero), [(0, 16)])
    row_sum = jnp.sum(total, axis=1, keepdims=True)
    inverse = 1.0 / row_sum
    att_own = (attended * inverse).astype(BF)
    grad = ob[0]
    row_delta = jnp.sum(grad.astype(F32) * att_own.astype(F32), axis=1, keepdims=True)
    row_lse = row_top + jnp.log2(row_sum)
    lane = lax.broadcasted_iota(jnp.int32, (HD, HD), 1)
    stat[0] = jnp.where(lane == 0, row_lse, jnp.where(lane == 1, row_delta, 0.0)).T[:8]
    att[0] = att_own
    s_line = []
    for cc in (0, 1):
        for dxi, who in ((0, 0), (2, 1), (1, -1), (3, 2)):
            if cc or dxi:
                s_line.append(send(stat.at[0], stat.at[4 * cc + dxi], at(dx=who, core=cc)))
    att_in = [send(att.at[0], att.at[dz], at(dz=-dz + nz)) for dz in range(1, nz)]

    ques.wave(2)
    grads.wave(3)
    grads.relay(2)
    grads.share(1)

    def slope(g, dq):
        d = nt(grad, chunk_b(vb, g))
        tiles = [
            (p_scr[g * 4 + b].astype(F32) * (d[:, b * HD:(b + 1) * HD] - row_delta)).astype(BF) for b in range(4)
        ]
        return dq + nn(jnp.concatenate(tiles, axis=1), chunk_a(ka, g))

    dq = over(slope, zero, [(0, 8)])
    arrive(*s_line)
    s_col = []
    for d in range(1, NY):
        slot = 1 if d == 4 else (2 * d + 1 if d < 4 else 2 * (NY - d))
        s_col.append(send(rows(stat, 0, 8), rows(stat, 8 * slot, 8), at(dy=d)))
    ques.wave(3)
    grads.wave(4)
    grads.relay(3)
    grads.share(2)
    grads.relay(4)
    dq = over(slope, dq, [(8, 8)])
    dq_ref[...] = (dq * (inverse * SCALE)).astype(BF)

    ques.last()
    grads.share(3)
    grads.share(0)

    k_own, v_own = ka[0], vb[0]

    def column(g, carry):
        dk, dv = carry
        queries, ograds = chunk_a(qa, g), chunk_b(ob, g)
        s, d = nt(k_own, queries), nt(v_own, ograds)
        probs, slopes = [], []
        for b in range(4):
            st = stat[(g % 8) * 8 + (g // 8) * 4 + b]
            shift = bias_of(mask_ref[place(g, b), own_seg]) - st[0:1]
            p = jnp.exp2(s[:, b * HD:(b + 1) * HD] * SCALE2 + shift)
            probs.append(p.astype(BF))
            slopes.append((p * (d[:, b * HD:(b + 1) * HD] - st[1:2])).astype(BF))
        dk = dk + nn(jnp.concatenate(slopes, axis=1), queries)
        dv = dv + nn(jnp.concatenate(probs, axis=1), ograds)
        return dk, dv

    arrive(*s_col)
    dkv = over(column, (zero, zero), [(0, 8)])
    arrive(*ques.sib, *grads.sib)
    dk, dv = over(column, dkv, [(8, 8)])
    dk_ref[...] = (dk * SCALE).astype(BF)
    dv_ref[...] = dv.astype(BF)

    out = nt(att_own, w_own[pl.ds(pl.multiple_of(z * ow, 16), ow)])
    arrive(*w_sib, *att_in)
    for dz in range(1, nz):
        out = out + nt(att[dz], w_all[dz])
    out_ref[...] = out.astype(BF)
    for cp in sent:
        cp.wait_send()


def solution(mesh):
    nz = mesh.shape["head"]

    def local(queries, keys, values, out_weight, output_cotangent, block_mask, segment_of_device):
        width = out_weight.shape[0]
        ow = width // nz
        anywhere, vmem, smem = (pl.BlockSpec(memory_space=m) for m in (pl.ANY, pltpu.VMEM, pltpu.SMEM))
        block = jax.ShapeDtypeStruct((HD, HD), BF)
        buf = pltpu.VMEM((BLOCKS, HD, HD), BF)
        return pl.pallas_call(
            functools.partial(kernel, nz, ow),
            out_shape=(jax.ShapeDtypeStruct((HD, ow), BF), block, block, block),
            in_specs=[anywhere] * 5 + [smem] * 2,
            out_specs=(vmem,) * 4,
            scratch_shapes=[
                buf, buf, buf, buf,
                pltpu.VMEM((BLOCKS, HD, HD), F32),
                pltpu.VMEM((BLOCKS, HD, HD), BF),
                pltpu.VMEM((width, HD), BF),
                pltpu.VMEM((HD, width), BF),
                pltpu.VMEM((nz, ow, HD), BF),
                pltpu.VMEM((nz, HD, HD), BF),
                pltpu.VMEM((BLOCKS, 8, HD), F32),
                pltpu.SemaphoreType.DMA((8,)),
                pltpu.SemaphoreType.DMA((160,)),
                pltpu.SemaphoreType.DMA((160,)),
            ],
            compiler_params=pltpu.CompilerParams(
                collective_id=0, has_side_effects=True, vmem_limit_bytes=48 * 1024 * 1024
            ),
        )(queries, keys, values, out_weight, output_cotangent, block_mask, segment_of_device)

    return jax.shard_map(
        local,
        mesh=mesh,
        in_specs=(P("tm", "head"), P("tm", "head"), P("tm", "head"), P(None, "head"), P("tm", None), P(), P()),
        out_specs=(P("tm", "head"), P("tm", "head"), P("tm", "head"), P("tm", "head")),
        check_vma=False,
    )
```

```python
import functools
import math

import jax
import jax.numpy as jnp
from jax import lax
from jax.experimental import pallas as pl
from jax.experimental.pallas import tpu as pltpu
from jax.sharding import PartitionSpec as P

HD = 128
NX, NY = 4, 8
BLOCKS = 2 * NX * NY
MASKED_SCORE = -1e30
SCALE = 1.0 / math.sqrt(HD)
SCALE2 = SCALE * math.log2(math.e)
MESH = pl.DeviceIdType.MESH
BF, F32 = jnp.bfloat16, jnp.float32

DX = (0, 1, -1, 2)
RIGHT, LEFT, ACROSS, UP, DOWN, SIB = (1, 0, 0), (-1, 0, 0), (2, 0, 0), (0, 1, 0), (0, -1, 0), (0, 0, 1)
TOP, LOW = pl.ds(0, 64), pl.ds(64, 64)
WAVES = (1, 2, 3, 0)

ROUTES = ((0, 1, True), (1, 0.5, 0), (0, 3, True), (1, 2.5, 1))
ORDER = (
    "Vy1 Vx0 Ky10 Kl", "Qy10 Gy2 Gx0 Ql", "Vy2 Vx1 Vr0 Ky20", "Ky12 Ky11 Ky13 Gr0",
    "Gx2 Vx2 Vy3 W", "Ky30 Ky22 Vr1 Ky21", "Ks1 Ky23 Vx3 Vy4", "Qy12 Ky40 Gr2 score1",
    "Qy20 Vr2 Ky32 Ky31", "Vs1 Ky33 Ks2 Vx4", "Vr3 Kf pv1 Gy3", "Gs2 score2 Vs2 Qy30",
    "Vr4 Gy1 Vs3 Ks3", "Qy13 pv2 Qy11 Gx4", "Qy22 Ks0 Gx3 Vs0", "Qy40 score3 Gx1 pv3",
    "Qy23 score0 Qy21 Gr4", "Qs1 pv0 stat Qf", "att Qy32 slope1 slope3", "Gr1 Qy33 Gs0 slope2",
    "Qs2 Qy31 Gr3 slope0", "dq scol Qs0 pre2", "Gs1 Gs3 Qs3 pre0", "pre1 col2 col0 w4",
    "w7 w3 w5 w2", "w6 w1 col1 pre3", "col3 dkv out",
)


class Route:
    def __init__(self, name, buf, post, send, rank):
        self.name, self.buf, self.rank = name, buf, rank
        self.post, self.send = post, send
        self.need, self.sib = {}, {}

    def move(self, src, dst, count, who, half=None):
        if half is not None:
            return self.send(self.buf, (src, half), (dst, half), who, count * 0.5)
        return self.send(self.buf, (pl.ds(src, count),), (pl.ds(dst, count),), who, count)

    def task(self, label, waits, work, rank=0.0):
        self.post(self.name + label, waits, work, self.rank + rank)

    def share(self):
        for p in WAVES:
            def work(p=p):
                return [self.move(8 * p, 32 + 8 * p, 8, SIB)]
            self.task("s%d" % p, self.need[p], work, 0.2)
            self.need[p] = self.need[p] + [self.name + "s%d.0" % p]


class RouteA(Route):
    def __init__(self, name, buf, post, send, rank, ready=(), far=False):
        super().__init__(name, buf, post, send, rank)
        ready, move = list(ready), self.move
        self.task("l", ready, lambda: [move(0, 2, 1, RIGHT), move(0, 1, 1, LEFT), move(0, 3, 1, ACROSS)])
        line = [ready, [name + "l.1"], [name + "l.0"], [name + "l.2"]]
        for p in (1, 2, 3):
            self.need[p] = []
        for d in range(4):
            def first(d=d):
                return [move(d, 12 + d, 1, UP), move(d, 8 + d, 1, DOWN)]
            self.task("y1%d" % d, line[d], first, 0.1)
            for p in (1, 2, 3):
                got = ["%sy%d%d.%d" % (name, p, d, i) for i in (0, 1)]
                self.need[p] += got
                if p < 3:
                    def more(d=d, g=8 * p):
                        return [move(g + 4 + d, g + 12 + d, 1, UP), move(g + d, g + 8 + d, 1, DOWN)]
                elif far and d:
                    continue
                elif far:
                    def more():
                        return [move(28, 4, 1, UP, TOP), move(24, 4, 1, DOWN, LOW)]
                else:
                    def more(d=d):
                        return [move(28 + d, 4 + d, 1, UP) if d < 2 else move(24 + d, 4 + d, 1, DOWN)]
                self.task("y%d%d" % (p + 1, d), got, more, 0.1)
        if far:
            self.task(
                "f", [name + "y40.0", name + "y40.1"],
                lambda: [move(4, 6, 1, RIGHT), move(4, 5, 1, LEFT), move(4, 7, 1, ACROSS)], 0.1
            )
            last = [name + "f.%d" % i for i in range(3)] + [name + "y40.0", name + "y40.1"]
        else:
            last = [name + "y4%d.0" % d for d in range(4)]
        self.need[0] = line[1] + line[2] + line[3] + last
        self.share()


class RouteB(Route):
    def __init__(self, name, buf, post, send, rank, ready=(), mode=0):
        super().__init__(name, buf, post, send, rank)
        ready, move = list(ready), self.move

        def to(p, src=0):
            return [move(src, 8 * p + 1, 1, (0, p, 0)), move(src, 8 * p, 1, (0, -p, 0))]

        got = {}
        if mode == 0:
            self.task("y1", ready, lambda: to(1))
            got[1] = [name + "y1.0", name + "y1.1"]
            for p in (1, 2, 3):
                if p < 3:
                    def work(g=8 * p):
                        return [move(g + 1, g + 9, 1, UP), move(g, g + 8, 1, DOWN)]
                else:
                    def work():
                        return [move(25, 1, 1, UP, TOP), move(24, 1, 1, DOWN, LOW)]
                self.task("y%d" % (p + 1), got[p], work)
                got[p + 1] = ["%sy%d.%d" % (name, p + 1, i) for i in (0, 1)]
        elif mode == 1:
            self.task("y2", ready, lambda: to(2))
            self.task("y1", ready, lambda: to(1), 0.01)
            got[1], got[2] = [name + "y1.0", name + "y1.1"], [name + "y2.0", name + "y2.1"]

            def work():
                return [
                    move(17, 1, 1, (0, 2, 0), TOP), move(16, 1, 1, (0, -2, 0), LOW),
                    move(17, 25, 1, UP), move(16, 24, 1, DOWN),
                ]
            self.task("y3", got[2], work)
            got[4], got[3] = [name + "y3.0", name + "y3.1"], [name + "y3.2", name + "y3.3"]
        else:
            self.task("y4", ready, lambda: [move(0, 1, 1, (0, 4, 0))])
            got[4] = [name + "y4.0"]
            for p in (3, 2, 1):
                self.task("y%d" % p, ready, lambda p=p: to(p), 0.01)
                got[p] = ["%sy%d.%d" % (name, p, i) for i in (0, 1)]
        got[0] = ready
        for p in (0, 1, 2, 3, 4):
            g, k, n = (8 * p, 0, 2) if 1 <= p <= 3 else (0, p // 4, 1)

            def cross(g=g, k=k, n=n):
                return [move(g + k, g + 4 + k, n, RIGHT), move(g + k, g + 2 + k, n, LEFT)]

            def relay(g=g, k=k, n=n):
                if n == 2:
                    return [move(g + 4, g + 6, 1, RIGHT), move(g + 3, g + 7, 1, LEFT)]
                return [move(4 + k, 6 + k, 1, RIGHT, TOP), move(2 + k, 6 + k, 1, LEFT, LOW)]

            self.task("x%d" % p, got[p], cross, 0.02)
            near = ["%sx%d.%d" % (name, p, i) for i in (0, 1)]
            self.task("r%d" % p, near, relay, 0.05)
            mine = (got[p] if p else []) + near + ["%sr%d.%d" % (name, p, i) for i in (0, 1)]
            self.need[p % 4] = self.need.get(p % 4, []) + mine
        self.share()


def routes(post, send, bufs, ready):
    made = []
    for (kind, rank, option), name, buf, dep in zip(ROUTES, "KVQG", bufs, ready):
        if kind:
            made.append(RouteB(name, buf, post, send, rank, dep, option))
        else:
            made.append(RouteA(name, buf, post, send, rank, dep, option))
    return [r.need for r in made]


def work_plan(post, send, bufs, act, nz):
    keys, vals, ques, grads = routes(post, send, bufs, ((), (), (), ()))
    w_in = []
    if nz > 1:
        post("W", ["Ky20.0"], act("W", 0), 0.9)
        for dz in range(1, nz):
            post("w%d" % dz, ["scol", "W.%d" % (dz - 1)], act("w", dz), 9.5)
            w_in += ["W.%d" % (dz - 1), "w%d.0" % dz]
    for p in WAVES:
        post("score%d" % p, keys[p], act("score", p), 10)
        post("pv%d" % p, vals[p] + ["score%d" % p], act("pv", p), 10.5)
        post("pre%d" % p, ques[p] + grads[p], act("pre", p), 13)
    post("stat", ["pv%d" % p for p in WAVES], act("stat", 0), 5)
    line = ["stat.%d" % i for i in range(7)]
    post("scol", line, act("scol", 0), 0)
    col = line + ["scol.%d" % i for i in range(NY - 1)]
    for p in WAVES:
        post("slope%d" % p, ["stat"], act("slope", p), 14)
        post("col%d" % p, col + ["pre%d" % p], act("col", p), 12)
    post("dq", ["slope%d" % p for p in WAVES], act("dq", 0), 15)
    post("dkv", ["col%d" % p for p in WAVES], act("dkv", 0), 11)
    if nz > 1:
        post("att", ["stat"], act("att", 0), 5.5)
    post("out", ["stat"] + w_in + ["att.%d" % i for i in range(nz - 1)], act("out", 0), 20)


def nt(left, right):
    return lax.dot_general(left, right, (((1,), (1,)), ((), ())), preferred_element_type=F32)


def nn(left, right):
    return lax.dot_general(left, right, (((1,), (0,)), ((), ())), preferred_element_type=F32)


def kernel(nz, ow, q_hbm, k_hbm, v_hbm, w_hbm, cot_hbm, mask_ref, seg_ref, out_ref, dq_ref, dk_ref, dv_ref,
           ka, vb, qa, ob, p_scr, s_scr, d_scr, w_own, cot, w_all, att, stat, lsem, ssem, rsem, go_sem):
    t, z = lax.axis_index("tm"), lax.axis_index("head")
    y, x, c = t // (2 * NX), (t // 2) % NX, t % 2

    def at(dx=0, dy=0, core=0, dz=0):
        col, row = (x + (dx + NX)) % NX, (y + (dy + NY)) % NY
        return ((row * NX + col) * 2 + (c + core) % 2, (z + (dz + nz)) % nz)

    loads = []
    for src, dst in ((w_hbm, w_own), (cot_hbm, cot), (k_hbm, ka.at[0]), (v_hbm, vb.at[0]), (q_hbm, qa.at[0])):
        cp = pltpu.make_async_copy(src, dst, lsem.at[len(loads)])
        cp.start()
        loads.append(cp)

    def signal(sem, who):
        pl.semaphore_signal(sem, inc=1, device_id=who, device_id_type=MESH)

    barrier = pltpu.get_barrier_semaphore()
    chips = [(dx, 0) for dx in DX[1:]] + [(0, dy) for dy in range(1, NY)]
    for dx, dy in chips:
        signal(barrier, at(dx, dy, c))

    @pl.when(c == 1)
    def _():
        signal(barrier, at(core=1))

    for cp in loads[:2]:
        cp.wait()
    grad = nn(cot[...], w_own[...]).astype(BF)
    ob[0] = grad
    for cp in loads[2:]:
        cp.wait()

    @pl.when(c == 0)
    def _():
        pl.semaphore_wait(barrier, 2 * len(chips) + 1)
        signal(go_sem, at(core=1))

    @pl.when(c == 1)
    def _():
        pl.semaphore_wait(go_sem, 1)
        for dz in range(1, nz):
            signal(barrier, at(dz=dz))

    sent, val = [], {}

    def push(src, dst, who):
        i = len(sent)
        cp = pltpu.make_async_remote_copy(
            src_ref=src, dst_ref=dst, send_sem=ssem.at[i], recv_sem=rsem.at[i], device_id=who, device_id_type=MESH
        )
        cp.start()
        sent.append(cp)
        return cp

    def send(buf, src, dst, who, count):
        return push(buf.at[src], buf.at[dst], at(*who))

    q_own, k_own, v_own = qa[0], ka[0], vb[0]
    own_seg = seg_ref[t]
    half = ow // 2
    part = pl.ds(pl.multiple_of(c * half, 16), half)

    def cells(p):
        return [(core, k, dxi) for core in (0, 1) for k in (0, 1) for dxi in range(4)]

    def place(p, core, k, dxi):
        dy = (4 * k) if p == 0 else (p if k == 0 else NY - p)
        col, row = (x + (DX[dxi] + NX)) % NX, (y + dy) % NY
        return seg_ref[(row * NX + col) * 2 + (c + core) % 2]

    def bias_of(link):
        return (1 - link).astype(F32) * MASKED_SCORE

    def chunk_a(buf, p):
        return jnp.concatenate([buf[pl.ds(32 * core + 8 * p, 8)].reshape(8 * HD, HD) for core in (0, 1)], axis=0)

    def chunk_b(buf, p):
        return jnp.concatenate([buf[32 * core + 8 * p + 2 * dxi + k] for core, k, dxi in cells(p)], axis=0)

    def score(p):
        s = nt(q_own, chunk_a(ka, p))
        tiles = []
        for i, cell in enumerate(cells(p)):
            bias = bias_of(mask_ref[own_seg, place(p, *cell)])
            tiles.append(s[:, i * HD:(i + 1) * HD] * SCALE2 + bias)
        top = functools.reduce(jnp.maximum, tiles)
        top = jnp.max(top, axis=1, keepdims=True)
        tiles = [jnp.exp2(tile - top) for tile in tiles]
        total = jnp.sum(functools.reduce(jnp.add, tiles), axis=1, keepdims=True)
        for i, tile in enumerate(tiles):
            p_scr[p * 16 + i] = tile.astype(BF)
        val["top", p], val["sum", p] = top, total

    def pv(p):
        val["pv", p] = nn(jnp.concatenate([p_scr[p * 16 + i] for i in range(16)], axis=1), chunk_b(vb, p))

    def finish(_):
        tops = [val["top", p] for p in WAVES]
        top = functools.reduce(jnp.maximum, tops)
        scale = {p: jnp.exp2(val["top", p] - top) for p in WAVES}
        row_sum = sum(val["sum", p] * scale[p] for p in WAVES)
        inverse = 1.0 / row_sum
        attended = (sum(val["pv", p] * scale[p] for p in WAVES) * inverse).astype(BF)
        delta = jnp.sum(grad.astype(F32) * attended.astype(F32), axis=1, keepdims=True)
        lse = top + jnp.log2(row_sum)
        lane = lax.broadcasted_iota(jnp.int32, (HD, HD), 1)
        stat[0] = jnp.where(lane == 0, lse, jnp.where(lane == 1, delta, 0.0)).T[:2]
        att[0] = attended
        val["att"], val["delta"] = attended, delta
        for p in WAVES:
            val["f", p] = scale[p] * (inverse * SCALE)
        return [
            push(stat.at[0], stat.at[4 * core + slot], at(dx=dx, core=core))
            for core in (0, 1) for slot, dx in ((0, 0), (2, 1), (1, -1), (3, 2)) if core or slot
        ]

    def spread(_):
        out = []
        for d in (4, 3, 5, 2, 6, 1, 7):
            slot = 1 if d == 4 else (2 * d + 1 if d < 4 else 2 * (NY - d))
            out.append(push(stat.at[pl.ds(0, 8)], stat.at[pl.ds(8 * slot, 8)], at(dy=d)))
        return out

    def slope(p):
        d = nt(grad, chunk_b(vb, p))
        tiles = [
            (p_scr[p * 16 + i].astype(F32) * (d[:, i * HD:(i + 1) * HD] - val["delta"])).astype(BF) for i in range(16)
        ]
        val["dq", p] = nn(jnp.concatenate(tiles, axis=1), chunk_a(ka, p)) * val["f", p]

    def put_dq(_):
        dq_ref[...] = sum(val["dq", p] for p in WAVES).astype(BF)

    def pre(p):
        s, d = nt(k_own, chunk_a(qa, p)), nt(v_own, chunk_b(ob, p))
        for i, cell in enumerate(cells(p)):
            bias = bias_of(mask_ref[place(p, *cell), own_seg])
            s_scr[p * 16 + i] = s[:, i * HD:(i + 1) * HD] * SCALE2 + bias
            d_scr[p * 16 + i] = d[:, i * HD:(i + 1) * HD]

    def col(p):
        probs, slopes = [], []
        for i, (core, k, dxi) in enumerate(cells(p)):
            st = stat[(2 * p + k) * 8 + core * 4 + dxi]
            e = jnp.exp2(s_scr[p * 16 + i] - st[0:1])
            probs.append(e.astype(BF))
            slopes.append((e * (d_scr[p * 16 + i] - st[1:2])).astype(BF))
        dk = nn(jnp.concatenate(slopes, axis=1), chunk_a(qa, p))
        dv = nn(jnp.concatenate(probs, axis=1), chunk_b(ob, p))
        val["dk"] = val["dk"] + dk if "dk" in val else dk
        val["dv"] = val["dv"] + dv if "dv" in val else dv

    def put_dkv(_):
        dk_ref[...] = (val["dk"] * SCALE).astype(BF)
        dv_ref[...] = val["dv"].astype(BF)

    def weights(_):
        out = []

        @pl.when(c == 1)
        def _():
            pl.semaphore_wait(barrier, nz - 1)
            signal(go_sem, at(core=1))

        @pl.when(c == 0)
        def _():
            pl.semaphore_wait(go_sem, 1)

        for dz in range(1, nz):
            first = pl.multiple_of(((z + nz - dz) % nz) * ow + c * half, 16)
            out.append(push(w_own.at[pl.ds(first, half)], w_all.at[dz, part], at(dz=-dz)))
        return out

    def weight(dz):
        return [push(w_all.at[dz, part], w_all.at[dz, part], at(core=1))]

    def heads(_):
        return [push(att.at[0], att.at[dz], at(dz=-dz)) for dz in range(1, nz)]

    def project(_):
        out = nt(val["att"], w_own[pl.ds(pl.multiple_of(z * ow, 16), ow)])
        for dz in range(1, nz):
            out = out + nt(att[dz], w_all[dz])
        out_ref[...] = out.astype(BF)

    acts = {
        "score": score, "pv": pv, "pre": pre, "stat": finish, "scol": spread, "slope": slope, "col": col, "dq": put_dq,
        "dkv": put_dkv, "W": weights, "w": weight, "att": heads, "out": project,
    }
    tasks = {}

    def post(name, waits, work, rank):
        tasks[name] = (waits, work)

    work_plan(post, send, (ka, vb, qa, ob), lambda kind, i: functools.partial(acts[kind], i), nz)
    names = [n for n in " ".join(ORDER).split() if n in tasks]
    assert sorted(names) == sorted(tasks)
    coming = {}
    for name in names:
        waits, work = tasks[name]
        for dep in waits:
            if "." in dep and coming[dep] is not None:
                coming[dep].wait_recv()
                coming[dep] = None
            elif "." not in dep:
                assert dep in tasks and names.index(dep) < names.index(name)
        for i, cp in enumerate(work() or ()):
            coming["%s.%d" % (name, i)] = cp
    assert all(cp is None for cp in coming.values())
    for cp in sent:
        cp.wait_send()


def hand_over(*refs):
    for i in range(4):
        refs[4 + i][...] = refs[i][...]


def solution(mesh):
    nz = mesh.shape["head"]

    def local(queries, keys, values, out_weight, output_cotangent, block_mask, segment_of_device):
        width = out_weight.shape[0]
        ow = width // nz
        anywhere, vmem, smem = (pl.BlockSpec(memory_space=m) for m in (pltpu.HBM, pltpu.VMEM, pltpu.SMEM))
        block = jax.ShapeDtypeStruct((HD, HD), BF)
        buf, big = pltpu.VMEM((BLOCKS, HD, HD), BF), pltpu.VMEM((BLOCKS, HD, HD), F32)
        shapes = (jax.ShapeDtypeStruct((HD, ow), BF), block, block, block)
        results = pl.pallas_call(
            functools.partial(kernel, nz, ow),
            out_shape=shapes,
            in_specs=[anywhere] * 5 + [smem] * 2,
            out_specs=(vmem,) * 4,
            scratch_shapes=[
                buf, buf, buf, buf, buf, big, big,
                pltpu.VMEM((width, HD), BF),
                pltpu.VMEM((HD, width), BF),
                pltpu.VMEM((nz, ow, HD), BF),
                pltpu.VMEM((nz, HD, HD), BF),
                pltpu.VMEM((BLOCKS, 2, HD), F32),
                pltpu.SemaphoreType.DMA((8,)),
                pltpu.SemaphoreType.DMA((240,)),
                pltpu.SemaphoreType.DMA((240,)),
                pltpu.SemaphoreType.REGULAR,
            ],
            compiler_params=pltpu.CompilerParams(
                collective_id=0, has_side_effects=True, vmem_limit_bytes=64 * 1024 * 1024
            ),
        )(queries, keys, values, out_weight, output_cotangent, block_mask, segment_of_device)
        return pl.pallas_call(
            hand_over,
            out_shape=shapes,
            in_specs=[vmem] * 4,
            out_specs=(vmem,) * 4,
            compiler_params=pltpu.CompilerParams(vmem_limit_bytes=64 * 1024 * 1024),
        )(*results)

    return jax.shard_map(
        local,
        mesh=mesh,
        in_specs=(P("tm", "head"), P("tm", "head"), P("tm", "head"), P(None, "head"), P("tm", None), P(), P()),
        out_specs=(P("tm", "head"), P("tm", "head"), P("tm", "head"), P("tm", "head")),
        check_vma=False,
    )
```

```python
import functools
import math

import jax
import jax.numpy as jnp
from jax import lax
from jax.experimental import pallas as pl
from jax.experimental.pallas import tpu as pltpu
from jax.sharding import PartitionSpec as P

HD = 128
NX, NY = 4, 8
BLOCKS = 2 * NX * NY
MASKED_SCORE = -1e30
SCALE = 1.0 / math.sqrt(HD)
SCALE2 = SCALE * math.log2(math.e)
MESH = pl.DeviceIdType.MESH
BF, F32 = jnp.bfloat16, jnp.float32

DX = (0, 1, -1, 2)
RIGHT, LEFT, ACROSS, UP, DOWN, SIB = (1, 0, 0), (-1, 0, 0), (2, 0, 0), (0, 1, 0), (0, -1, 0), (0, 0, 1)
TOP, LOW = pl.ds(0, 64), pl.ds(64, 64)
WAVES = (1, 2, 3, 0)


def far_first(nz):
    return sorted(range(1, nz), key=lambda dz: -min(dz, nz - dz))

NEAR = (1, -1, 2, -2)
ROUTES = ((0, 1, 1), (1, 0.5, 1), (0, 3, 1), (1, 2.5, 0))
ORDER = (
    1, 0, 40, 24, 23, 26, 63, 2, 5, 28, 67, 8, 11, 30, 25, 27, 3, 61, 64, 69, 29, 9, 12, 6,
    81, 34, 41, 32, 15, 4, 31, 65, 71, 16, 10, 36, 13, 17, 7, 35, 18, 21, 42, 14, 48, 51, 33, 70,
    89, 37, 66, 45, 92, 20, 90, 72, 73, 19, 43, 39, 93, 22, 49, 52, 68, 75, 38, 95, 46, 98, 44, 99,
    96, 101, 113, 50, 76, 77, 56, 55, 74, 47, 105, 53, 54, 107, 114, 78, 58, 103, 57, 102, 109, 80, 111, 91,
    79, 59, 94, 60, 62, 104, 84, 83, 87, 82, 86, 88, 85, 106, 97, 100, 108, 115, 110, 116, 117, 112, 119, 118,
    120, 121, 122,
)


class Route:
    def __init__(self, name, buf, post, send, rank):
        self.name, self.buf, self.rank = name, buf, rank
        self.post, self.send = post, send
        self.need, self.sib = {}, {}

    def move(self, src, dst, count, who, half=None):
        if half is not None:
            return self.send(self.buf, (src, half), (dst, half), who, count * 0.5)
        return self.send(self.buf, (pl.ds(src, count),), (pl.ds(dst, count),), who, count)

    def task(self, label, waits, work, rank=0.0):
        self.post(self.name + label, waits, work, self.rank + rank)

    def share(self, split):
        for p in WAVES:
            for i, waits in enumerate(self.need[p] if split else [self.need[p]]):
                def work(start=8 * p + 4 * i, count=4 if split else 8):
                    return [self.move(start, 32 + start, count, SIB)]
                self.task("s%d%d" % (p, i), waits, work, 0.2)
            if split:
                self.need[p] = self.need[p][0] + self.need[p][1] + ["%ss%d%d.0" % (self.name, p, i) for i in (0, 1)]
            else:
                self.need[p] = self.need[p] + ["%ss%d0.0" % (self.name, p)]


class RouteA(Route):
    def __init__(self, name, buf, post, send, rank, ready=(), far=False):
        super().__init__(name, buf, post, send, rank)
        ready, move = list(ready), self.move
        self.task("l", ready, lambda: [move(0, 2, 1, RIGHT), move(0, 1, 1, LEFT), move(0, 3, 1, ACROSS)])
        line = [ready, [name + "l.1"], [name + "l.0"], [name + "l.2"]]
        for p in (1, 2, 3):
            self.need[p] = ([], [])
        for d in range(4 if far == 3 else 0):
            def two(d=d):
                return [move(d, 20 + d, 1, (0, 2, 0)), move(d, 16 + d, 1, (0, -2, 0))]

            def one(d=d):
                return [move(d, 12 + d, 1, UP), move(d, 8 + d, 1, DOWN)]

            def three(d=d):
                return [move(20 + d, 28 + d, 1, UP), move(16 + d, 24 + d, 1, DOWN)]
            got = ["%sy2%d.%d" % (name, d, i) for i in (0, 1)]
            self.task("y2%d" % d, line[d], two, 0.1)
            self.task("y1%d" % d, line[d], one, 0.11)
            self.task("y3%d" % d, got, three, 0.1)
            for p in (1, 2, 3):
                for i in (0, 1):
                    self.need[p][1 - i].append("%sy%d%d.%d" % (name, p, d, i))
        for d in range(0 if far == 3 else 4):
            def first(d=d):
                return [move(d, 12 + d, 1, UP), move(d, 8 + d, 1, DOWN)]
            self.task("y1%d" % d, line[d], first, 0.1)
            for p in (1, 2, 3):
                got = ["%sy%d%d.%d" % (name, p, d, i) for i in (0, 1)]
                for i in (0, 1):
                    self.need[p][1 - i].append(got[i])
                if p < 3:
                    def more(d=d, g=8 * p):
                        return [move(g + 4 + d, g + 12 + d, 1, UP), move(g + d, g + 8 + d, 1, DOWN)]
                elif far and d:
                    continue
                elif far == 2:
                    continue
                elif far:
                    def more():
                        return [move(28, 4, 1, UP, TOP), move(24, 4, 1, DOWN, LOW)]
                else:
                    def more(d=d):
                        return [move(28 + d, 4 + d, 1, UP) if d < 2 else move(24 + d, 4 + d, 1, DOWN)]
                self.task("y%d%d" % (p + 1, d), got, more, 0.1)
        if far:
            end = [name + "y40.0", name + "y40.1"][:1 if far > 1 else 2]
            if far > 1:
                self.task("y40", ready, lambda: [move(0, 4, 1, (0, 4, 0))], 0.15)
            self.task(
                "f", end,
                lambda: [move(4, 6, 1, RIGHT), move(4, 5, 1, LEFT), move(4, 7, 1, ACROSS)], 0.1
            )
            last = [name + "f.%d" % i for i in range(3)] + end
        else:
            last = [name + "y4%d.0" % d for d in range(4)]
        self.need[0] = (line[1] + line[2] + line[3], last)
        self.share(True)


class RouteB(Route):
    def __init__(self, name, buf, post, send, rank, ready=(), mode=0):
        super().__init__(name, buf, post, send, rank)
        ready, move = list(ready), self.move

        def to(p, src=0):
            return [move(src, 8 * p + 1, 1, (0, p, 0)), move(src, 8 * p, 1, (0, -p, 0))]

        got = {}
        if mode >= 3:
            self.task("y4", ready, lambda: [move(0, 1, 1, (0, 4, 0))], 0.15)
            got[4] = [name + "y4.0"]
        if mode == 4:
            self.task("y2", ready, lambda: to(2), 0.01)
            self.task("y1", ready, lambda: to(1), 0.02)
            got[1], got[2] = [name + "y1.0", name + "y1.1"], [name + "y2.0", name + "y2.1"]
            self.task("y3", got[2], lambda: [move(17, 25, 1, UP), move(16, 24, 1, DOWN)])
            got[3] = [name + "y3.0", name + "y3.1"]
        elif mode in (0, 3):
            self.task("y1", ready, lambda: to(1))
            got[1] = [name + "y1.0", name + "y1.1"]
            for p in (1, 2) if mode else (1, 2, 3):
                if p < 3:
                    def work(g=8 * p):
                        return [move(g + 1, g + 9, 1, UP), move(g, g + 8, 1, DOWN)]
                else:
                    def work():
                        return [move(25, 1, 1, UP, TOP), move(24, 1, 1, DOWN, LOW)]
                self.task("y%d" % (p + 1), got[p], work)
                got[p + 1] = ["%sy%d.%d" % (name, p + 1, i) for i in (0, 1)]
        elif mode == 1:
            self.task("y2", ready, lambda: to(2))
            self.task("y1", ready, lambda: to(1), 0.01)
            got[1], got[2] = [name + "y1.0", name + "y1.1"], [name + "y2.0", name + "y2.1"]

            def work():
                return [
                    move(17, 1, 1, (0, 2, 0), TOP), move(16, 1, 1, (0, -2, 0), LOW),
                    move(17, 25, 1, UP), move(16, 24, 1, DOWN),
                ]
            self.task("y3", got[2], work)
            got[4], got[3] = [name + "y3.0", name + "y3.1"], [name + "y3.2", name + "y3.3"]
        else:
            self.task("y4", ready, lambda: [move(0, 1, 1, (0, 4, 0))])
            got[4] = [name + "y4.0"]
            for p in (3, 2, 1):
                self.task("y%d" % p, ready, lambda p=p: to(p), 0.01)
                got[p] = ["%sy%d.%d" % (name, p, i) for i in (0, 1)]
        got[0] = ready
        for p in (0, 1, 2, 3, 4):
            g, k, n = (8 * p, 0, 2) if 1 <= p <= 3 else (0, p // 4, 1)

            def cross(g=g, k=k, n=n):
                return [move(g + k, g + 4 + k, n, RIGHT), move(g + k, g + 2 + k, n, LEFT)]

            def relay(g=g, k=k, n=n):
                if n == 2:
                    return [move(g + 4, g + 6, 1, RIGHT), move(g + 3, g + 7, 1, LEFT)]
                return [move(4 + k, 6 + k, 1, RIGHT, TOP), move(2 + k, 6 + k, 1, LEFT, LOW)]

            self.task("x%d" % p, got[p], cross, 0.02)
            near = ["%sx%d.%d" % (name, p, i) for i in (0, 1)]
            self.task("r%d" % p, near, relay, 0.05)
            mine = (got[p] if p else []) + near + ["%sr%d.%d" % (name, p, i) for i in (0, 1)]
            self.need[p % 4] = self.need.get(p % 4, []) + mine
        self.share(False)


def routes(post, send, bufs, ready):
    made = []
    for (kind, rank, option), name, buf, dep in zip(ROUTES, "KVQG", bufs, ready):
        if kind:
            made.append(RouteB(name, buf, post, send, rank, dep, option))
        else:
            made.append(RouteA(name, buf, post, send, rank, dep, option))
    return [r.need for r in made]


def work_plan(post, send, bufs, act, nz):
    keys, vals, ques, grads = routes(post, send, bufs, ((), (), (), ()))
    others = far_first(nz)
    if nz > 1:
        post("W", ["Ky20.0"], act("W", 0), 0.9)
    for i, dz in enumerate(others):
        post("w%d" % dz, ["col1", "dq", "W.%d" % i], act("w", dz), 11.5)
    for p in WAVES:
        post("score%d" % p, keys[p], act("score", p), 10)
        post("pv%d" % p, vals[p] + ["score%d" % p], act("pv", p), 10.5)
        post("pre%d" % p, ques[p] + grads[p], act("pre", p), 13)
    post("stat", ["pv%d" % p for p in WAVES], act("stat", 0), 5)
    line = ["stat.%d" % i for i in range(7)]
    post("scol", line, act("scol", 0), 0)
    for p in WAVES:
        post("slope%d" % p, ["stat"], act("slope", p), 14)
        post("col%d" % p, line + (["scol.%d" % (2 * p - 2), "scol.%d" % (2 * p - 1)] if p else ["scol.6"]) + ["pre%d" % p], act("col", p), 12)
    post("dq", ["slope%d" % p for p in WAVES], act("dq", 0), 15)
    post("dkv", ["col%d" % p for p in WAVES], act("dkv", 0), 11)
    if nz > 1:
        post("att", ["stat"], act("att", 0), 5.5)
    post("out0", ["stat"], act("out", 0), 16)
    for i, dz in enumerate(others):
        post("out%d" % dz, ["out0", "W.%d" % i, "w%d.0" % dz, "att.%d" % i], act("out", dz), 20)
    post("put", ["out%d" % dz for dz in [0] + others], act("put", 0), 21)


def nt(left, right):
    return lax.dot_general(left, right, (((1,), (1,)), ((), ())), preferred_element_type=F32)


def nn(left, right):
    return lax.dot_general(left, right, (((1,), (0,)), ((), ())), preferred_element_type=F32)


def kernel(nz, ow, q_hbm, k_hbm, v_hbm, w_hbm, cot_hbm, mask_ref, seg_ref, out_ref, dq_ref, dk_ref, dv_ref,
           ka, vb, qa, ob, p_scr, s_scr, d_scr, w_own, cot, w_all, att, stat, lsem, ssem, rsem, go_sem):
    t, z = lax.axis_index("tm"), lax.axis_index("head")
    y, x, c = t // (2 * NX), (t // 2) % NX, t % 2

    def at(dx=0, dy=0, core=0, dz=0):
        col, row = (x + (dx + NX)) % NX, (y + (dy + NY)) % NY
        return ((row * NX + col) * 2 + (c + core) % 2, (z + (dz + nz)) % nz)

    loads = []
    for src, dst in ((w_hbm, w_own), (cot_hbm, cot), (k_hbm, ka.at[0]), (v_hbm, vb.at[0]), (q_hbm, qa.at[0])):
        cp = pltpu.make_async_copy(src, dst, lsem.at[len(loads)])
        cp.start()
        loads.append(cp)

    def signal(sem, who):
        pl.semaphore_signal(sem, inc=1, device_id=who, device_id_type=MESH)

    barrier = pltpu.get_barrier_semaphore()
    chips = [(dx, 0) for dx in DX[1:]] + [(0, dy) for dy in NEAR]
    for dx, dy in chips:
        signal(barrier, at(dx, dy, c))

    @pl.when(c == 1)
    def _():
        signal(barrier, at(core=1))

    for cp in loads[:2]:
        cp.wait()
    grad = nn(cot[...], w_own[...]).astype(BF)
    ob[0] = grad
    for cp in loads[2:]:
        cp.wait()

    @pl.when(c == 0)
    def _():
        pl.semaphore_wait(barrier, 2 * len(chips) + 1)
        signal(go_sem, at(core=1))

    @pl.when(c == 1)
    def _():
        pl.semaphore_wait(go_sem, 1)
        for dz in range(1, nz):
            signal(barrier, at(dz=dz))

    sent, val = [], {}

    def push(src, dst, who):
        i = len(sent)
        cp = pltpu.make_async_remote_copy(
            src_ref=src, dst_ref=dst, send_sem=ssem.at[i], recv_sem=rsem.at[i], device_id=who, device_id_type=MESH
        )
        cp.start()
        sent.append(cp)
        return cp

    def send(buf, src, dst, who, count):
        return push(buf.at[src], buf.at[dst], at(*who))

    q_own, k_own, v_own = qa[0], ka[0], vb[0]
    own_seg = seg_ref[t]
    half = ow // 2
    part = pl.ds(pl.multiple_of(c * half, 16), half)

    def cells(p):
        return [(core, k, dxi) for core in (0, 1) for k in (0, 1) for dxi in range(4)]

    def place(p, core, k, dxi):
        dy = (4 * k) if p == 0 else (p if k == 0 else NY - p)
        col, row = (x + (DX[dxi] + NX)) % NX, (y + dy) % NY
        return seg_ref[(row * NX + col) * 2 + (c + core) % 2]

    def bias_of(link):
        return (1 - link).astype(F32) * MASKED_SCORE

    def chunk_a(buf, p):
        return jnp.concatenate([buf[pl.ds(32 * core + 8 * p, 8)].reshape(8 * HD, HD) for core in (0, 1)], axis=0)

    def chunk_b(buf, p):
        return jnp.concatenate([buf[32 * core + 8 * p + 2 * dxi + k] for core, k, dxi in cells(p)], axis=0)

    def score(p):
        s = nt(q_own, chunk_a(ka, p))
        tiles = []
        for i, cell in enumerate(cells(p)):
            bias = bias_of(mask_ref[own_seg, place(p, *cell)])
            tiles.append(s[:, i * HD:(i + 1) * HD] * SCALE2 + bias)
        top = functools.reduce(jnp.maximum, tiles)
        top = jnp.max(top, axis=1, keepdims=True)
        tiles = [jnp.exp2(tile - top) for tile in tiles]
        total = jnp.sum(functools.reduce(jnp.add, tiles), axis=1, keepdims=True)
        for i, tile in enumerate(tiles):
            p_scr[p * 16 + i] = tile.astype(BF)
        val["top", p], val["sum", p] = top, total

    def pv(p):
        val["pv", p] = nn(jnp.concatenate([p_scr[p * 16 + i] for i in range(16)], axis=1), chunk_b(vb, p))

    def finish(_):
        tops = [val["top", p] for p in WAVES]
        top = functools.reduce(jnp.maximum, tops)
        scale = {p: jnp.exp2(val["top", p] - top) for p in WAVES}
        row_sum = sum(val["sum", p] * scale[p] for p in WAVES)
        inverse = 1.0 / row_sum
        attended = (sum(val["pv", p] * scale[p] for p in WAVES) * inverse).astype(BF)
        delta = jnp.sum(grad.astype(F32) * attended.astype(F32), axis=1, keepdims=True)
        lse = top + jnp.log2(row_sum)
        lane = lax.broadcasted_iota(jnp.int32, (HD, HD), 1)
        stat[0] = jnp.where(lane == 0, lse, jnp.where(lane == 1, delta, 0.0)).T[:2]
        att[0] = attended
        val["att"], val["delta"] = attended, delta
        for p in WAVES:
            val["f", p] = scale[p] * (inverse * SCALE)
        return [
            push(stat.at[0], stat.at[4 * core + slot], at(dx=dx, core=core))
            for core in (0, 1) for slot, dx in ((0, 0), (2, 1), (1, -1), (3, 2)) if core or slot
        ]

    def spread(_):
        out = []
        for p in WAVES:
            if p:
                out.append(push(stat.at[pl.ds(0, 8)], stat.at[pl.ds(16 * p + 8, 8)], at(dy=p)))
                out.append(push(stat.at[pl.ds(0, 8)], stat.at[pl.ds(16 * p, 8)], at(dy=-p)))
            else:
                out.append(push(stat.at[pl.ds(0, 8)], stat.at[pl.ds(8, 8)], at(dy=4)))
        return out

    def slope(p):
        d = nt(grad, chunk_b(vb, p))
        tiles = [
            (p_scr[p * 16 + i].astype(F32) * (d[:, i * HD:(i + 1) * HD] - val["delta"])).astype(BF) for i in range(16)
        ]
        val["dq", p] = nn(jnp.concatenate(tiles, axis=1), chunk_a(ka, p)) * val["f", p]

    def put_dq(_):
        dq_ref[...] = sum(val["dq", p] for p in WAVES).astype(BF)

    def pre(p):
        s, d = nt(k_own, chunk_a(qa, p)), nt(v_own, chunk_b(ob, p))
        for i, cell in enumerate(cells(p)):
            bias = bias_of(mask_ref[place(p, *cell), own_seg])
            s_scr[p * 16 + i] = s[:, i * HD:(i + 1) * HD] * SCALE2 + bias
            d_scr[p * 16 + i] = d[:, i * HD:(i + 1) * HD]

    def col(p):
        probs, slopes = [], []
        for i, (core, k, dxi) in enumerate(cells(p)):
            st = stat[16 * p + 8 * k + 4 * core + dxi]
            e = jnp.exp2(s_scr[p * 16 + i] - st[0:1])
            probs.append(e.astype(BF))
            slopes.append((e * (d_scr[p * 16 + i] - st[1:2])).astype(BF))
        dk = nn(jnp.concatenate(slopes, axis=1), chunk_a(qa, p))
        dv = nn(jnp.concatenate(probs, axis=1), chunk_b(ob, p))
        val["dk"] = val["dk"] + dk if "dk" in val else dk
        val["dv"] = val["dv"] + dv if "dv" in val else dv

    def put_dkv(_):
        dk_ref[...] = (val["dk"] * SCALE).astype(BF)
        dv_ref[...] = val["dv"].astype(BF)

    def weights(_):
        out = []

        @pl.when(c == 1)
        def _():
            pl.semaphore_wait(barrier, nz - 1)
            signal(go_sem, at(core=1))

        @pl.when(c == 0)
        def _():
            pl.semaphore_wait(go_sem, 1)

        for dz in far_first(nz):
            first = pl.multiple_of(((z + nz - dz) % nz) * ow + c * half, 16)
            out.append(push(w_own.at[pl.ds(first, half)], w_all.at[dz, part], at(dz=-dz)))
        return out

    def weight(dz):
        return [push(w_all.at[dz, part], w_all.at[dz, part], at(core=1))]

    def heads(_):
        return [push(att.at[0], att.at[dz], at(dz=-dz)) for dz in far_first(nz)]

    def project(dz):
        if dz:
            val["out"] = val["out"] + nt(att[dz], w_all[dz])
        else:
            val["out"] = nt(val["att"], w_own[pl.ds(pl.multiple_of(z * ow, 16), ow)])

    def put_out(_):
        out_ref[...] = val["out"].astype(BF)

    acts = {
        "score": score, "pv": pv, "pre": pre, "stat": finish, "scol": spread, "slope": slope, "col": col, "dq": put_dq,
        "dkv": put_dkv, "W": weights, "w": weight, "att": heads, "out": project, "put": put_out,
    }
    tasks = {}

    def post(name, waits, work, rank):
        tasks[name] = (waits, work)

    work_plan(post, send, (ka, vb, qa, ob), lambda kind, i: functools.partial(acts[kind], i), nz)
    names = [list(tasks)[i] for i in ORDER]
    assert sorted(names) == sorted(tasks)
    coming = {}
    for name in names:
        waits, work = tasks[name]
        for dep in waits:
            if "." in dep and coming[dep] is not None:
                coming[dep].wait_recv()
                coming[dep] = None
            elif "." not in dep:
                assert dep in tasks and names.index(dep) < names.index(name)
        for i, cp in enumerate(work() or ()):
            coming["%s.%d" % (name, i)] = cp
    assert all(cp is None for cp in coming.values())
    for cp in sent:
        cp.wait_send()


def hand_over(*refs):
    for i in range(4):
        refs[4 + i][...] = refs[i][...]


def solution(mesh):
    nz = mesh.shape["head"]

    def local(queries, keys, values, out_weight, output_cotangent, block_mask, segment_of_device):
        width = out_weight.shape[0]
        ow = width // nz
        anywhere, vmem, smem = (pl.BlockSpec(memory_space=m) for m in (pltpu.HBM, pltpu.VMEM, pltpu.SMEM))
        block = jax.ShapeDtypeStruct((HD, HD), BF)
        buf, big = pltpu.VMEM((BLOCKS, HD, HD), BF), pltpu.VMEM((BLOCKS, HD, HD), F32)
        shapes = (jax.ShapeDtypeStruct((HD, ow), BF), block, block, block)
        results = pl.pallas_call(
            functools.partial(kernel, nz, ow),
            out_shape=shapes,
            in_specs=[anywhere] * 5 + [smem] * 2,
            out_specs=(vmem,) * 4,
            scratch_shapes=[
                buf, buf, buf, buf, buf, big, big,
                pltpu.VMEM((width, HD), BF),
                pltpu.VMEM((HD, width), BF),
                pltpu.VMEM((nz, ow, HD), BF),
                pltpu.VMEM((nz, HD, HD), BF),
                pltpu.VMEM((BLOCKS, 2, HD), F32),
                pltpu.SemaphoreType.DMA((8,)),
                pltpu.SemaphoreType.DMA((240,)),
                pltpu.SemaphoreType.DMA((240,)),
                pltpu.SemaphoreType.REGULAR,
            ],
            compiler_params=pltpu.CompilerParams(
                collective_id=0, has_side_effects=True, vmem_limit_bytes=64 * 1024 * 1024
            ),
        )(queries, keys, values, out_weight, output_cotangent, block_mask, segment_of_device)
        return pl.pallas_call(
            hand_over,
            out_shape=shapes,
            in_specs=[vmem] * 4,
            out_specs=(vmem,) * 4,
            compiler_params=pltpu.CompilerParams(vmem_limit_bytes=64 * 1024 * 1024),
        )(*results)

    return jax.shard_map(
        local,
        mesh=mesh,
        in_specs=(P("tm", "head"), P("tm", "head"), P("tm", "head"), P(None, "head"), P("tm", None), P(), P()),
        out_specs=(P("tm", "head"), P("tm", "head"), P("tm", "head"), P("tm", "head")),
        check_vma=False,
    )
```
